32 devices in a mesh: seq: 4 (over y, x), req: 8 (over z, core).
Axes of the slice: x: 2, y: 2, z: 4, core: 2. Of those that a mesh axis runs over, the one named last changes fastest.
Arguments:
- stream_tokens: bfloat16 [16384, 2048], P(('seq', 'req')), may hold values from -6 to 6
- xbc_weight: bfloat16 [2048, 5120], P(None, ('seq', 'req')), may hold values from -0.125 to 0.125
- step_weight: bfloat16 [2048, 64], replicated, may hold values from -0.125 to 0.125
- conv_weight: float32 [4, 5120], replicated, may hold values from -3 to 3
- conv_bias: float32 [5120], replicated, may hold values from -3 to 3
- step_bias: float32 [64], replicated, may hold values from -6 to -4
- decay_rate: float32 [64], replicated, may hold values from 0.02 to 3
- skip_gain: float32 [64], replicated, may hold values from 0.1 to 0.5
- norm_gain: float32 [4096], replicated, may hold values from 0.5 to 1.5
- segment_ids: int32 [8, 2048], P('req'), may hold values from 0 to 1, never falling along the last dimension, each value on 1 to 1536 neighbouring positions
- page_target: int32 [32, 8], P(('seq', 'req')), may hold values from 0 to 7, each once within a row
Outputs:
- mixer_out: bfloat16 [16384, 4096], P(('seq', 'req'))
The draws below stay inside these ranges and needn't reach their ends.
Inputs may be any that keep to these rules, and one draw needn't show every extreme that they name: `segment_ids`: along each row the ids never fall; each request holds 512 to 1536 consecutive tokens. `page_target`: each row holds every request group's index once.
All inputs are finite; a program needn't handle non-finite values.
Results may differ from the reference program's by a relative error of at most 0.0066.
Values may be sent and summed in bfloat16 or wider, within the bound.
A program may use at most 128 MiB of HBM per device.

```python
import math
from functools import partial
import jax
import jax.numpy as jnp
import numpy as np
from jax import lax

D = 2048
HEADS = 64
HEAD_DIM = 64
GROUPS = 4
STATE = 128
KCONV = 4
SPAN = 256
SEGS = 2
TOK_DEV = 512
INNER = 4096
XBC = 5120
PAGE = 64
TOKENS = 16384
N_SEQ = 4
N_REQ = 8


def levels(rng, extent, cuts, smallest, high):
    def one(axis_at, blocks):
        steps = jax.random.uniform(jax.random.fold_in(jax.random.fold_in(rng, 6), axis_at), (blocks,), jnp.float32, smallest / len(cuts), high / len(cuts))
        return jnp.repeat(jnp.exp(steps), extent[axis_at] // blocks).reshape((-1,) + (1,) * (len(extent) - axis_at - 1))

    loudness = one(*cuts[0])
    for cut in cuts[1:]:
        loudness = loudness * one(*cut)
    return loudness


def profile(number_of, total, most, slope):
    loads = [(1 << 20) // math.isqrt(rank ** slope) + 1 for rank in range(2, number_of + 1)]
    rest, holding = total - most - (number_of - 1), [1] * (number_of - 1)
    while rest > 0:
        movable = [i for i in range(number_of - 1) if holding[i] < most]
        pool, budget = sum([loads[i] for i in movable]), rest
        for i in movable:
            more = min(most - holding[i], max(1, budget * loads[i] // pool), rest)
            holding[i] = holding[i] + more
            rest = rest - more
    return np.array([most] + holding)


def uneven(key, amount, total, limit, lean):
    if amount == 2:
        one = jax.random.randint(key, (), max(1, total - limit), min(limit, total - 1) + 1)
        return jnp.stack([one, total - one])
    sizes = jnp.asarray(profile(amount, total, limit, lean), jnp.int32)
    pairs = (amount - 1) // 2
    donor, taker = sizes[1:1 + 2 * pairs:2], sizes[2:2 + 2 * pairs:2]
    slack = jnp.minimum(donor - 1, limit - taker)
    moved = jax.random.randint(jax.random.fold_in(key, 1), (pairs,), 0, 1 << 20) % (slack + 1)
    sizes = sizes.at[1:1 + 2 * pairs:2].set(donor - moved).at[2:2 + 2 * pairs:2].set(taker + moved)
    return sizes[jax.random.permutation(jax.random.fold_in(key, 2), amount)]


def bell_draw(own_key, dims, scale, bound, shards=(), kind=jnp.bfloat16):
    drawn = jax.random.normal(own_key, dims, jnp.float32) * scale
    if len(shards) > 0:
        drawn = levels(own_key, dims, shards, -0.22, 0.18) * drawn
    return jnp.clip(drawn, min=-bound, max=bound).astype(kind)


def setup_inputs(seed: int = 0) -> dict:
    key_list = jax.random.split(jax.random.key(seed), 12)
    return {
        "stream_tokens": bell_draw(key_list[0], (TOKENS, D), 1.0, 6.0, ((0, 32),)),
        "xbc_weight": bell_draw(key_list[1], (D, XBC), D ** -0.5, 0.125, ((1, 32),)),
        "step_weight": bell_draw(key_list[2], (D, HEADS), D ** -0.5, 0.125),
        "conv_weight": bell_draw(key_list[3], (KCONV, XBC), KCONV ** -0.5, 3.0, (), jnp.float32),
        "conv_bias": bell_draw(key_list[4], (XBC,), 0.5, 3.0, (), jnp.float32),
        "step_bias": jnp.clip(jax.random.uniform(key_list[5], (HEADS,), jnp.float32, -6.0, -4.0), -6.0, -4.0),
        "decay_rate": jnp.clip(jnp.exp(jax.random.uniform(key_list[6], (HEADS,), jnp.float32, math.log(0.02), math.log(3.0))), 0.02, 3.0),
        "skip_gain": jnp.clip(jax.random.uniform(key_list[7], (HEADS,), jnp.float32, 0.1, 0.5), 0.1, 0.5),
        "norm_gain": jnp.clip(1.0 + 0.1 * jax.random.normal(key_list[8], (INNER,), jnp.float32), 0.5, 1.5),
        "segment_ids": jax.vmap(lambda own: jnp.searchsorted(jnp.cumsum(uneven(own, SEGS, N_SEQ * TOK_DEV, 3 * TOK_DEV, 2)), jnp.arange(N_SEQ * TOK_DEV), side="right"))(jax.random.split(key_list[9], N_REQ)).reshape((N_REQ, N_SEQ * TOK_DEV)).astype(jnp.int32),
        "page_target": jax.vmap(lambda own: jax.random.permutation(own, N_REQ))(jax.random.split(key_list[10], (N_SEQ * N_REQ))).reshape((N_SEQ * N_REQ, N_REQ)).astype(jnp.int32),
    }


def conv_rows(raw_rows, seg_rows, prev_raw, prev_seg, conv_weight, conv_bias):
    conv_taps = conv_weight.shape[0]
    row_count = raw_rows.shape[0]
    stacked = jnp.concatenate([prev_raw, raw_rows], axis=0).astype(jnp.float32)
    labels = jnp.concatenate([prev_seg, seg_rows], axis=0)
    summed = conv_bias[None, :] + conv_weight[conv_taps - 1][None, :] * stacked[conv_taps - 1:]
    for offset in range(conv_taps - 1):
        matching = (labels[offset:offset + row_count] == seg_rows).astype(jnp.float32)
        summed = summed + conv_weight[offset][None, :] * stacked[offset:offset + row_count] * matching[:, None]
    return jax.nn.silu(summed).astype(jnp.bfloat16)

def span_step(decay_rate, state, pieces):
    x_heads, b_mat, c_mat, step_size, seg_rows, seg_before = pieces
    span_len, head_count, head_dim = x_heads.shape
    group_count, state_dim = (b_mat.shape[1], b_mat.shape[2])
    per_group = head_count // group_count
    log_decay = jnp.cumsum(-step_size * decay_rate[None, :], axis=0)
    places = jnp.arange(span_len)
    allowed = (seg_rows[:, None] == seg_rows[None, :]) & (places[:, None] >= places[None, :])
    scores = jnp.einsum('tgn,ugn->gtu', c_mat.astype(jnp.float32), b_mat.astype(jnp.float32))
    spread = log_decay.T[:, :, None] - log_decay.T[:, None, :]
    decays = jnp.where(allowed[None], jnp.exp(jnp.where(allowed[None], spread, 0.0)), 0.0)
    mixing = (scores.reshape(group_count, 1, span_len, span_len) * decays.reshape(group_count, per_group, span_len, span_len) * step_size.T.reshape(group_count, per_group, 1, span_len)).astype(jnp.bfloat16)
    inside = jnp.einsum('ghtu,ughp->tghp', mixing.astype(jnp.float32), x_heads.reshape(span_len, group_count, per_group, head_dim).astype(jnp.float32))
    keeping = (seg_rows == seg_before).astype(jnp.float32)
    readout = jnp.einsum('tgn,ghpn->tghp', c_mat.astype(jnp.float32), state.reshape(group_count, per_group, head_dim, state_dim), precision=lax.Precision.HIGHEST)
    carried = readout * (keeping[:, None] * jnp.exp(log_decay)).reshape(span_len, group_count, per_group, 1)
    final_seg = seg_rows[span_len - 1]
    tail_weight = jnp.where(seg_rows[:, None] == final_seg, jnp.exp(log_decay[span_len - 1][None, :] - log_decay), 0.0) * step_size
    weighted = (x_heads.astype(jnp.float32) * tail_weight[:, :, None]).astype(jnp.bfloat16)
    gained = jnp.einsum('ughp,ugn->ghpn', weighted.reshape(span_len, group_count, per_group, head_dim).astype(jnp.float32), b_mat.astype(jnp.float32))
    passing = jnp.where(final_seg == seg_before, jnp.exp(log_decay[span_len - 1]), 0.0)
    new_state = passing[:, None, None] * state + gained.reshape(head_count, head_dim, state_dim)
    return (new_state, (inside + carried).reshape(span_len, head_count * head_dim))

def normalize(mixed_rows, x_heads, skip_gain, norm_gain):
    combined = mixed_rows + (x_heads.astype(jnp.float32) * skip_gain[None, :, None]).reshape(mixed_rows.shape)
    power = lax.optimization_barrier(jnp.mean(combined * combined, axis=-1, keepdims=True))
    return (combined * lax.rsqrt(power + 1e-05) * norm_gain[None, :]).astype(jnp.bfloat16)

def group_pass(token_rows, seg_rows, xbc_weight, step_weight, conv_weight, conv_bias, step_bias, decay_rate, skip_gain, norm_gain):
    raw_rows = jnp.dot(token_rows, xbc_weight, preferred_element_type=jnp.float32).astype(jnp.bfloat16)
    step_raw = jnp.dot(token_rows, step_weight, preferred_element_type=jnp.float32).astype(jnp.bfloat16)
    conv_out = conv_rows(raw_rows, seg_rows, jnp.zeros((KCONV - 1, XBC), jnp.bfloat16), jnp.full((KCONV - 1,), -1, jnp.int32), conv_weight, conv_bias)
    step_size = jax.nn.softplus(step_raw.astype(jnp.float32) + step_bias[None, :])
    row_count = token_rows.shape[0]
    x_heads = conv_out[:, :INNER].reshape(row_count, HEADS, HEAD_DIM)
    b_mat = conv_out[:, INNER:INNER + GROUPS * STATE].reshape(row_count, GROUPS, STATE)
    c_mat = conv_out[:, INNER + GROUPS * STATE:].reshape(row_count, GROUPS, STATE)
    blocks = row_count // SPAN
    block_ends = seg_rows.reshape(blocks, SPAN)[:, SPAN - 1]
    before = jnp.concatenate([jnp.full((1,), -1, jnp.int32), block_ends[:-1].astype(jnp.int32)])
    pieces = (x_heads.reshape(blocks, SPAN, HEADS, HEAD_DIM), b_mat.reshape(blocks, SPAN, GROUPS, STATE), c_mat.reshape(blocks, SPAN, GROUPS, STATE), step_size.reshape(blocks, SPAN, HEADS), seg_rows.reshape(blocks, SPAN), before)
    _, outputs = lax.scan(partial(span_step, decay_rate), jnp.zeros((HEADS, HEAD_DIM, STATE), jnp.float32), pieces)
    return normalize(outputs.reshape(row_count, INNER), x_heads, skip_gain, norm_gain)

def reference(stream_tokens, xbc_weight, step_weight, conv_weight, conv_bias, step_bias, decay_rate, skip_gain, norm_gain, segment_ids, page_target):
    inverse = jnp.argsort(page_target, axis=1).astype(jnp.int32)
    page_blocks = stream_tokens.reshape(N_SEQ, N_REQ, N_REQ, PAGE, D)
    picked = jnp.take_along_axis(page_blocks, inverse.reshape(N_SEQ, N_REQ, N_REQ, 1, 1), axis=2)
    layout = picked.transpose(2, 0, 1, 3, 4).reshape(N_REQ, N_SEQ * TOK_DEV, D)

    def one_group(packed):
        return group_pass(packed[0], packed[1], xbc_weight, step_weight, conv_weight, conv_bias, step_bias, decay_rate, skip_gain, norm_gain)
    mixed_rows = lax.map(one_group, (layout, segment_ids))
    grouped = mixed_rows.reshape(N_REQ, N_SEQ, N_REQ, PAGE, INNER).transpose(1, 2, 0, 3, 4)
    restored = jnp.take_along_axis(grouped, page_target.reshape(N_SEQ, N_REQ, N_REQ, 1, 1), axis=2)
    return restored.reshape(TOKENS, INNER)
```

```python
from functools import partial

import jax
import jax.numpy as jnp
from jax import lax
from jax.sharding import PartitionSpec as P

HEADS = 64
HEAD_DIM = 64
GROUPS = 4
STATE = 128
KCONV = 4
SPAN = 256
INNER = 4096
XBC = 5120


def shifted(shard, axis, by):
    peers = lax.axis_size(axis)
    pairs = [(i, i + by) for i in range(peers) if 0 <= i + by < peers]
    return lax.ppermute(shard, axis, pairs)


def conv_rows(raw_rows, seg_rows, prev_raw, prev_seg, conv_weight, conv_bias):
    conv_taps = conv_weight.shape[0]
    row_count = raw_rows.shape[0]
    stacked = jnp.concatenate([prev_raw, raw_rows], axis=0).astype(jnp.float32)
    labels = jnp.concatenate([prev_seg, seg_rows], axis=0)
    summed = conv_bias[None, :] + conv_weight[conv_taps - 1][None, :] * stacked[conv_taps - 1 :]
    for offset in range(conv_taps - 1):
        matching = (labels[offset : offset + row_count] == seg_rows).astype(jnp.float32)
        summed = (
            summed
            + conv_weight[offset][None, :]
            * stacked[offset : offset + row_count]
            * matching[:, None]
        )
    return jax.nn.silu(summed).astype(jnp.bfloat16)


def state_readout(c_mat, state_four):
    upper = state_four.astype(jnp.bfloat16)
    lower = (state_four - upper.astype(jnp.float32)).astype(jnp.bfloat16)
    first = jnp.einsum("tgn,ghpn->tghp", c_mat, upper, preferred_element_type=jnp.float32)
    second = jnp.einsum("tgn,ghpn->tghp", c_mat, lower, preferred_element_type=jnp.float32)
    return first + second


def span_step(decay_rate, state, pieces):
    x_heads, b_mat, c_mat, step_size, seg_rows, seg_before = pieces
    span_len, head_count, head_dim = x_heads.shape
    group_count, state_dim = (b_mat.shape[1], b_mat.shape[2])
    per_group = head_count // group_count
    log_decay = jnp.cumsum(-step_size * decay_rate[None, :], axis=0)
    places = jnp.arange(span_len)
    allowed = (seg_rows[:, None] == seg_rows[None, :]) & (places[:, None] >= places[None, :])
    scores = jnp.einsum("tgn,ugn->gtu", c_mat, b_mat, preferred_element_type=jnp.float32)
    spread = log_decay.T[:, :, None] - log_decay.T[:, None, :]
    decays = jnp.where(allowed[None], jnp.exp(jnp.where(allowed[None], spread, 0.0)), 0.0)
    mixing = (
        scores.reshape(group_count, 1, span_len, span_len)
        * decays.reshape(group_count, per_group, span_len, span_len)
        * step_size.T.reshape(group_count, per_group, 1, span_len)
    ).astype(jnp.bfloat16)
    inside = jnp.einsum(
        "ghtu,ughp->tghp",
        mixing,
        x_heads.reshape(span_len, group_count, per_group, head_dim),
        preferred_element_type=jnp.float32,
    )
    keeping = (seg_rows == seg_before).astype(jnp.float32)
    readout = state_readout(c_mat, state.reshape(group_count, per_group, head_dim, state_dim))
    carried = readout * (keeping[:, None] * jnp.exp(log_decay)).reshape(
        span_len, group_count, per_group, 1
    )
    final_seg = seg_rows[span_len - 1]
    tail_weight = (
        jnp.where(
            seg_rows[:, None] == final_seg,
            jnp.exp(log_decay[span_len - 1][None, :] - log_decay),
            0.0,
        )
        * step_size
    )
    weighted = (x_heads.astype(jnp.float32) * tail_weight[:, :, None]).astype(jnp.bfloat16)
    gained = jnp.einsum(
        "ughp,ugn->ghpn",
        weighted.reshape(span_len, group_count, per_group, head_dim),
        b_mat,
        preferred_element_type=jnp.float32,
    )
    passing = jnp.where(final_seg == seg_before, jnp.exp(log_decay[span_len - 1]), 0.0)
    new_state = passing[:, None, None] * state + gained.reshape(head_count, head_dim, state_dim)
    return (new_state, (inside + carried).reshape(span_len, head_count * head_dim))


def normalize(mixed_rows, x_heads, skip_gain, norm_gain):
    combined = mixed_rows + (x_heads.astype(jnp.float32) * skip_gain[None, :, None]).reshape(
        mixed_rows.shape
    )
    power = jnp.mean(combined * combined, axis=-1, keepdims=True)
    return (combined * lax.rsqrt(power + 1e-05) * norm_gain[None, :]).astype(jnp.bfloat16)


HALO = 16


def per_device(
    stream_tokens,
    xbc_weight,
    step_weight,
    conv_weight,
    conv_bias,
    step_bias,
    decay_rate,
    skip_gain,
    norm_gain,
    segment_ids,
    page_target,
):
    req_count = lax.axis_size("req")
    seq_count = lax.axis_size("seq")
    tok_rows = stream_tokens.shape[0]
    page_rows = tok_rows // req_count
    targets = page_target[0]
    spots = jnp.arange(req_count, dtype=jnp.int32)
    page_order = jnp.sum(jnp.where(targets[None, :] == spots[:, None], spots[None, :], 0), axis=1)
    per_group = HEADS // GROUPS
    in_bounds = "clip"

    pages = stream_tokens.reshape(req_count, page_rows, stream_tokens.shape[1])
    outgoing = jnp.take(pages, page_order, axis=0, mode=in_bounds)
    tokens = lax.all_to_all(outgoing, "req", split_axis=0, concat_axis=0, tiled=True)
    tokens = tokens.reshape(tok_rows, stream_tokens.shape[1])
    prev_tokens = shifted(tokens[tok_rows - HALO :], "seq", 1)
    full_weight = lax.all_gather(xbc_weight, ("seq", "req"), axis=1, tiled=True)
    all_rows = jnp.concatenate([prev_tokens, tokens], axis=0)
    raw_all = jnp.dot(all_rows, full_weight, preferred_element_type=jnp.float32).astype(
        jnp.bfloat16
    )
    step_raw = jnp.dot(tokens, step_weight, preferred_element_type=jnp.float32).astype(jnp.bfloat16)
    prev_raw, raw_rows = (raw_all[HALO - (KCONV - 1) : HALO], raw_all[HALO:])

    seq_at = lax.axis_index("seq")
    full_ids = segment_ids[0]
    padded_ids = jnp.concatenate([jnp.full((KCONV - 1,), -1, jnp.int32), full_ids])
    seg_rows = lax.dynamic_slice_in_dim(full_ids, seq_at * tok_rows, tok_rows)
    prev_ids = lax.dynamic_slice_in_dim(padded_ids, seq_at * tok_rows, KCONV - 1)
    seg_before = prev_ids[KCONV - 2]
    conv_out = conv_rows(raw_rows, seg_rows, prev_raw, prev_ids, conv_weight, conv_bias)
    step_size = jax.nn.softplus(step_raw.astype(jnp.float32) + step_bias[None, :])
    x_heads = conv_out[:, :INNER].reshape(tok_rows, HEADS, HEAD_DIM)
    b_mat = conv_out[:, INNER : INNER + GROUPS * STATE].reshape(tok_rows, GROUPS, STATE)
    c_mat = conv_out[:, INNER + GROUPS * STATE :].reshape(tok_rows, GROUPS, STATE)
    blocks = tok_rows // SPAN
    block_ends = seg_rows.reshape(blocks, SPAN)[:, SPAN - 1]
    before = jnp.concatenate([seg_before[None], block_ends[:-1]])
    pieces = (
        x_heads.reshape(blocks, SPAN, HEADS, HEAD_DIM),
        b_mat.reshape(blocks, SPAN, GROUPS, STATE),
        c_mat.reshape(blocks, SPAN, GROUPS, STATE),
        step_size.reshape(blocks, SPAN, HEADS),
        seg_rows.reshape(blocks, SPAN),
        before,
    )
    local_state, outputs = lax.scan(
        partial(span_step, decay_rate), jnp.zeros((HEADS, HEAD_DIM, STATE), jnp.float32), pieces
    )
    log_decay = jnp.cumsum(-step_size * decay_rate[None, :], axis=0)
    through = jnp.where(seg_rows[tok_rows - 1] == seg_before, jnp.exp(log_decay[tok_rows - 1]), 0.0)
    all_states = lax.all_gather(local_state.astype(jnp.bfloat16), "seq")
    all_through = lax.all_gather(through, "seq")
    incoming = jnp.zeros((HEADS, HEAD_DIM, STATE), jnp.float32)
    running = jnp.ones((HEADS,), jnp.float32)
    for turn in range(seq_count - 2, -1, -1):
        used = (turn < seq_at).astype(jnp.float32)
        incoming = incoming + (used * running)[:, None, None] * all_states[turn].astype(jnp.float32)
        running = jnp.where(turn < seq_at, running * all_through[turn], running)
    readout = state_readout(c_mat, incoming.reshape(GROUPS, per_group, HEAD_DIM, STATE))
    keeping = (seg_rows == seg_before).astype(jnp.float32)
    factor = keeping[:, None] * jnp.exp(log_decay)
    mixed_rows = outputs.reshape(tok_rows, INNER) + (
        readout * factor.reshape(tok_rows, GROUPS, per_group, 1)
    ).reshape(tok_rows, INNER)
    normed = normalize(mixed_rows, x_heads, skip_gain, norm_gain)
    returned = lax.all_to_all(
        normed.reshape(req_count, page_rows, INNER), "req", split_axis=0, concat_axis=0, tiled=True
    )
    return jnp.take(returned, targets, axis=0, mode=in_bounds).reshape(tok_rows, INNER)


def solution(mesh):
    in_specs = (
        P(("seq", "req"), None),
        P(None, ("seq", "req")),
        P(),
        P(),
        P(),
        P(),
        P(),
        P(),
        P(),
        P("req", None),
        P(("seq", "req"), None),
    )
    out_specs = P(("seq", "req"), None)
    return jax.shard_map(
        per_device, mesh=mesh, in_specs=in_specs, out_specs=out_specs, check_vma=False
    )
```

```python
from functools import partial

import jax
import jax.numpy as jnp
from jax import lax
from jax.experimental import pallas as pl
from jax.experimental.pallas import tpu as pltpu
from jax.sharding import PartitionSpec as P

HEADS = 64
HEAD_DIM = 64
GROUPS = 4
STATE = 128
KCONV = 4
SPAN = 256
INNER = 4096
XBC = 5120


def shifted(shard, axis, by):
    peers = lax.axis_size(axis)
    pairs = [(i, i + by) for i in range(peers) if 0 <= i + by < peers]
    return lax.ppermute(shard, axis, pairs)


HALO = 16
PER_GROUP = HEADS // GROUPS
WIDE = PER_GROUP * HEAD_DIM
LANES = 128
VMEM_LIMIT = 40 * 1024 * 1024


def dot32(left, right, contract=((1,), (0,))):
    return lax.dot_general(left, right, (contract, ((), ())), preferred_element_type=jnp.float32)


def conv_kernel(
    raw_x, raw_b, raw_c, w_x, w_b, w_c, bias_x, bias_b, bias_c, match, tail, pass_last, expand,
    x_out, b_out, c_out, first_state, last_state, wide,
):
    rows = x_out.shape[0]
    piece = 64

    def conv(raw, weight, bias, out):
        wide[:, : raw.shape[1]] = raw[...].astype(jnp.float32)

        @pl.loop(0, raw.shape[1] // LANES)
        def _(chunk):
            cols = pl.ds(pl.multiple_of(chunk * LANES, LANES), LANES)
            taps = weight[:, cols]
            shift = bias[:, cols]
            for start in range(0, rows, piece):
                base = HALO + start
                total = shift + taps[KCONV - 1 : KCONV] * wide[base : base + piece, cols]
                for tap in range(KCONV - 1):
                    low = base - (KCONV - 1) + tap
                    total = total + (
                        taps[tap : tap + 1]
                        * wide[low : low + piece, cols]
                        * match[tap, start : start + piece, :]
                    )
                out[start : start + piece, cols] = (total / (1.0 + jnp.exp(-total))).astype(
                    jnp.bfloat16
                )

    conv(raw_x, w_x, bias_x, x_out)
    conv(raw_b, w_b, bias_b, b_out)
    conv(raw_c, w_c, bias_c, c_out)
    gains = []
    for start in range(0, rows, SPAN):
        part = slice(start, start + SPAN)
        factor = dot32(tail[0, part, :], expand[...])
        weighted = (x_out[part, :].astype(jnp.float32) * factor).astype(jnp.bfloat16)
        gains.append(dot32(b_out[part, :], weighted, ((0,), (0,))))
    first_state[0] = gains[0]
    last_state[0] = (gains[0] * pass_last[0] + gains[1]).astype(jnp.bfloat16)


def mix_kernel(x_ref, b_ref, c_ref, decay_col, decay_row, step_row, seg_col, seg_row, out, scores):
    rows = x_ref.shape[0]
    lanes = lax.broadcasted_iota(jnp.int32, (SPAN, LANES), 1)
    for start in range(0, rows, SPAN):
        part = slice(start, start + SPAN)
        at_row = lax.broadcasted_iota(jnp.int32, (SPAN, SPAN), 0)
        at_col = lax.broadcasted_iota(jnp.int32, (SPAN, SPAN), 1)
        allowed = (seg_col[part, :] == seg_row[:, part]) & (at_row >= at_col)
        products = dot32(c_ref[part, :], b_ref[part, :], ((1,), (1,)))
        scores[...] = jnp.where(allowed, products, 0.0)
        for pair in range(PER_GROUP // 2):
            cols = slice(pair * LANES, (pair + 1) * LANES)
            values = x_ref[part, cols]
            halves = []
            for head in (2 * pair, 2 * pair + 1):
                spread = decay_col[0, part, head : head + 1] - decay_row[0, head : head + 1, part]
                mixing = (
                    scores[...] * jnp.exp(jnp.minimum(spread, 0.0)) * step_row[0, head : head + 1, part]
                ).astype(jnp.bfloat16)
                halves.append(dot32(mixing, values))
            out[part, cols] = jnp.where(lanes < HEAD_DIM, halves[0], halves[1])


def norm_kernel(inside, x_ref, c_ref, upper, lower, factor, expand, skip, gain, out, mixed):
    power = jnp.zeros((out.shape[0], 1), jnp.float32)
    for group in range(GROUPS):
        cols = slice(group * WIDE, (group + 1) * WIDE)
        c_mat = c_ref[:, group * STATE : (group + 1) * STATE]
        readout = dot32(c_mat, upper[0, group]) + dot32(c_mat, lower[0, group])
        total = inside[:, cols] + readout * dot32(factor[group], expand[...])
        total = total + x_ref[:, cols].astype(jnp.float32) * skip[:, cols]
        mixed[:, cols] = total
        power = power + jnp.sum(total * total, axis=1, keepdims=True)
    scale = lax.rsqrt(power / INNER + 1e-05)
    for group in range(GROUPS):
        cols = slice(group * WIDE, (group + 1) * WIDE)
        out[:, cols] = (mixed[:, cols] * scale * gain[:, cols]).astype(jnp.bfloat16)


def by_group(values):
    return values.reshape(values.shape[0], GROUPS, PER_GROUP).transpose(1, 0, 2)


def split_pair(values):
    grouped = by_group(values)
    upper = grouped.astype(jnp.bfloat16)
    lower = (grouped - upper.astype(jnp.float32)).astype(jnp.bfloat16)
    return jnp.concatenate([upper, lower], axis=2)


def along_lanes(values):
    return jnp.repeat(values, HEAD_DIM, axis=-1).reshape(values.shape[:-1] + (GROUPS, 1, WIDE))


def per_device(
    stream_tokens,
    xbc_weight,
    step_weight,
    conv_weight,
    conv_bias,
    step_bias,
    decay_rate,
    skip_gain,
    norm_gain,
    segment_ids,
    page_target,
):
    req_count = lax.axis_size("req")
    seq_count = lax.axis_size("seq")
    tok_rows = stream_tokens.shape[0]
    page_rows = tok_rows // req_count
    blocks = tok_rows // SPAN
    targets = page_target[0]
    spots = jnp.arange(req_count, dtype=jnp.int32)
    page_order = jnp.sum(jnp.where(targets[None, :] == spots[:, None], spots[None, :], 0), axis=1)
    params = pltpu.CompilerParams(vmem_limit_bytes=VMEM_LIMIT)

    pages = stream_tokens.reshape(req_count, page_rows, stream_tokens.shape[1])
    outgoing = jnp.take(pages, page_order, axis=0, mode="clip")
    tokens = lax.all_to_all(outgoing, "req", split_axis=0, concat_axis=0, tiled=True)
    tokens = tokens.reshape(tok_rows, stream_tokens.shape[1])
    prev_tokens = shifted(tokens[tok_rows - HALO :], "seq", 1)
    full_weight = lax.all_gather(xbc_weight, ("seq", "req"), axis=1, tiled=True)
    all_rows = jnp.concatenate([prev_tokens, tokens], axis=0)
    raw_all = jnp.dot(all_rows, full_weight, preferred_element_type=jnp.float32).astype(
        jnp.bfloat16
    )
    step_raw = jnp.dot(tokens, step_weight, preferred_element_type=jnp.float32).astype(jnp.bfloat16)

    seq_at = lax.axis_index("seq")
    full_ids = segment_ids[0]
    padded_ids = jnp.concatenate([jnp.full((KCONV - 1,), -1, jnp.int32), full_ids])
    labels = lax.dynamic_slice_in_dim(padded_ids, seq_at * tok_rows, tok_rows + KCONV - 1)
    seg_rows = labels[KCONV - 1 :]
    match = jnp.stack([labels[tap : tap + tok_rows] == seg_rows for tap in range(KCONV - 1)])
    match = jnp.broadcast_to(match.astype(jnp.float32)[:, :, None], (KCONV - 1, tok_rows, LANES))
    ends = seg_rows.reshape(blocks, SPAN)[:, SPAN - 1]
    before = jnp.concatenate([labels[KCONV - 2 : KCONV - 1], ends[:-1]])

    step_size = jax.nn.softplus(step_raw.astype(jnp.float32) + step_bias[None, :])
    log_decay = jnp.cumsum(
        (-step_size * decay_rate[None, :]).reshape(blocks, SPAN, HEADS), axis=1
    )
    last_decay = log_decay[:, SPAN - 1]
    seg_blocks = seg_rows.reshape(blocks, SPAN)
    keep = (seg_blocks == before[:, None])[:, :, None]
    factor = split_pair(jnp.where(keep, jnp.exp(log_decay), 0.0).reshape(tok_rows, HEADS))
    in_tail = (seg_blocks == ends[:, None])[:, :, None]
    tail = jnp.where(in_tail, jnp.exp(last_decay[:, None] - log_decay), 0.0).reshape(tok_rows, HEADS)
    tail = split_pair(tail * step_size)
    passing = jnp.where((ends == before)[:, None], jnp.exp(last_decay), 0.0)
    all_through = lax.all_gather(passing[0] * passing[1], "seq")
    running = jnp.ones((HEADS,), jnp.float32)
    shares = [None] * seq_count
    for turn in range(seq_count - 1, -1, -1):
        shares[turn] = jnp.where(turn < seq_at, running, 0.0)
        running = jnp.where(turn < seq_at, running * all_through[turn], running)
    shares = along_lanes(jnp.stack(shares))
    passing = along_lanes(passing)
    flat_decay = log_decay.reshape(tok_rows, HEADS)
    decay_col = by_group(flat_decay)
    decay_row = flat_decay.T.reshape(GROUPS, PER_GROUP, tok_rows)
    step_row = step_size.T.reshape(GROUPS, PER_GROUP, tok_rows)
    owner = jnp.arange(WIDE) // HEAD_DIM
    expand = (owner[None, :] == (jnp.arange(2 * PER_GROUP) % PER_GROUP)[:, None]).astype(
        jnp.bfloat16
    )

    bias_row = conv_bias[None, :]
    at_b = INNER // STATE
    at_c = at_b + GROUPS
    raw_len = tok_rows + HALO

    def columns(height, width, at):
        return pl.BlockSpec((height, width), lambda group: (0, at + group))

    def of_group(*shape):
        return pl.BlockSpec((1,) + shape, lambda group: (group, 0, 0))

    def whole(*shape):
        return pl.BlockSpec(shape, lambda step: (0,) * len(shape))

    x_all, b_all, c_all, first_state, last_state = pl.pallas_call(
        conv_kernel,
        grid=(GROUPS,),
        in_specs=[
            columns(raw_len, WIDE, 0),
            columns(raw_len, STATE, at_b),
            columns(raw_len, STATE, at_c),
            columns(KCONV, WIDE, 0),
            columns(KCONV, STATE, at_b),
            columns(KCONV, STATE, at_c),
            columns(1, WIDE, 0),
            columns(1, STATE, at_b),
            columns(1, STATE, at_c),
            whole(KCONV - 1, tok_rows, LANES),
            of_group(tok_rows, 2 * PER_GROUP),
            of_group(1, WIDE),
            whole(2 * PER_GROUP, WIDE),
        ],
        out_specs=[
            columns(tok_rows, WIDE, 0),
            columns(tok_rows, STATE, 0),
            columns(tok_rows, STATE, 0),
            of_group(STATE, WIDE),
            of_group(STATE, WIDE),
        ],
        out_shape=[
            jax.ShapeDtypeStruct((tok_rows, INNER), jnp.bfloat16),
            jax.ShapeDtypeStruct((tok_rows, GROUPS * STATE), jnp.bfloat16),
            jax.ShapeDtypeStruct((tok_rows, GROUPS * STATE), jnp.bfloat16),
            jax.ShapeDtypeStruct((GROUPS, STATE, WIDE), jnp.float32),
            jax.ShapeDtypeStruct((GROUPS, STATE, WIDE), jnp.bfloat16),
        ],
        scratch_shapes=[pltpu.VMEM((raw_len, WIDE), jnp.float32)],
        compiler_params=params,
        cost_estimate=pl.CostEstimate(
            flops=2 * tok_rows * INNER * STATE, bytes_accessed=14 << 20, transcendentals=tok_rows * XBC
        ),
    )(
        raw_all, raw_all, raw_all, conv_weight, conv_weight, conv_weight,
        bias_row, bias_row, bias_row, match, tail, passing[1], expand,
    )
    all_states = lax.all_gather(last_state, "seq")

    inside = pl.pallas_call(
        mix_kernel,
        grid=(GROUPS,),
        in_specs=[
            columns(tok_rows, WIDE, 0),
            columns(tok_rows, STATE, 0),
            columns(tok_rows, STATE, 0),
            of_group(tok_rows, PER_GROUP),
            of_group(PER_GROUP, tok_rows),
            of_group(PER_GROUP, tok_rows),
            whole(tok_rows, 1),
            whole(1, tok_rows),
        ],
        out_specs=columns(tok_rows, WIDE, 0),
        out_shape=jax.ShapeDtypeStruct((tok_rows, INNER), jnp.float32),
        scratch_shapes=[pltpu.VMEM((SPAN, SPAN), jnp.float32)],
        compiler_params=params,
        cost_estimate=pl.CostEstimate(
            flops=16 * tok_rows * SPAN * INNER,
            bytes_accessed=14 << 20,
            transcendentals=tok_rows * SPAN * HEADS,
        ),
    )(x_all, b_all, c_all, decay_col, decay_row, step_row, seg_rows[:, None], seg_rows[None, :])

    incoming = jnp.sum(shares * all_states.astype(jnp.float32), axis=0)
    states = jnp.stack([incoming, passing[0] * incoming + first_state])
    upper = states.astype(jnp.bfloat16)
    lower = (states - upper.astype(jnp.float32)).astype(jnp.bfloat16)

    tile = SPAN // 2
    per_block = SPAN // tile
    normed = pl.pallas_call(
        norm_kernel,
        grid=(tok_rows // tile,),
        in_specs=[
            pl.BlockSpec((tile, INNER), lambda step: (step, 0)),
            pl.BlockSpec((tile, INNER), lambda step: (step, 0)),
            pl.BlockSpec((tile, GROUPS * STATE), lambda step: (step, 0)),
            pl.BlockSpec((1, GROUPS, STATE, WIDE), lambda step: (step // per_block, 0, 0, 0)),
            pl.BlockSpec((1, GROUPS, STATE, WIDE), lambda step: (step // per_block, 0, 0, 0)),
            pl.BlockSpec((GROUPS, tile, 2 * PER_GROUP), lambda step: (0, step, 0)),
            whole(2 * PER_GROUP, WIDE),
            whole(1, INNER),
            whole(1, INNER),
        ],
        out_specs=pl.BlockSpec((tile, INNER), lambda step: (step, 0)),
        out_shape=jax.ShapeDtypeStruct((tok_rows, INNER), jnp.bfloat16),
        scratch_shapes=[pltpu.VMEM((tile, INNER), jnp.float32)],
        compiler_params=params,
        cost_estimate=pl.CostEstimate(
            flops=4 * tok_rows * INNER * STATE, bytes_accessed=22 << 20, transcendentals=tok_rows
        ),
    )(
        inside, x_all, c_all, upper, lower, factor, expand,
        jnp.repeat(skip_gain, HEAD_DIM)[None, :], norm_gain[None, :],
    )
    returned = lax.all_to_all(
        normed.reshape(req_count, page_rows, INNER), "req", split_axis=0, concat_axis=0, tiled=True
    )
    return jnp.take(returned, targets, axis=0, mode="clip").reshape(tok_rows, INNER)


def solution(mesh):
    in_specs = (
        P(("seq", "req"), None),
        P(None, ("seq", "req")),
        P(),
        P(),
        P(),
        P(),
        P(),
        P(),
        P(),
        P("req", None),
        P(("seq", "req"), None),
    )
    out_specs = P(("seq", "req"), None)
    return jax.shard_map(
        per_device, mesh=mesh, in_specs=in_specs, out_specs=out_specs, check_vma=False
    )
```

```python
from functools import partial

import jax
import jax.numpy as jnp
from jax import lax
from jax.experimental import pallas as pl
from jax.experimental.pallas import tpu as pltpu
from jax.sharding import PartitionSpec as P

HEADS = 64
HEAD_DIM = 64
GROUPS = 4
STATE = 128
KCONV = 4
SPAN = 256
INNER = 4096
XBC = 5120


def shifted(shard, axis, by):
    peers = lax.axis_size(axis)
    pairs = [(i, i + by) for i in range(peers) if 0 <= i + by < peers]
    return lax.ppermute(shard, axis, pairs)


HALO = 16
PER_GROUP = HEADS // GROUPS
WIDE = PER_GROUP * HEAD_DIM
LANES = 128
VMEM_LIMIT = 40 * 1024 * 1024


def dot32(left, right, contract=((1,), (0,))):
    return lax.dot_general(left, right, (contract, ((), ())), preferred_element_type=jnp.float32)


def conv_kernel(
    raw_x, raw_b, raw_c, w_x, w_b, w_c, bias_x, bias_b, bias_c, match, tail, pass_last, through, expand,
    x_out, b_out, c_out, first_state, last_state, wide,
):
    rows = x_out.shape[0]
    piece = 64

    def conv(raw, weight, bias, out):
        wide[:, : raw.shape[1]] = raw[...].astype(jnp.float32)

        @pl.loop(0, raw.shape[1] // LANES)
        def _(chunk):
            cols = pl.ds(pl.multiple_of(chunk * LANES, LANES), LANES)
            taps = weight[:, cols]
            shift = bias[:, cols]
            for start in range(0, rows, piece):
                base = HALO + start
                total = shift + taps[KCONV - 1 : KCONV] * wide[base : base + piece, cols]
                for tap in range(KCONV - 1):
                    low = base - (KCONV - 1) + tap
                    total = total + (
                        taps[tap : tap + 1]
                        * wide[low : low + piece, cols]
                        * match[tap, start : start + piece, :]
                    )
                out[start : start + piece, cols] = (total / (1.0 + jnp.exp(-total))).astype(
                    jnp.bfloat16
                )

    conv(raw_x, w_x, bias_x, x_out)
    conv(raw_b, w_b, bias_b, b_out)
    conv(raw_c, w_c, bias_c, c_out)
    gains = []
    for start in range(0, rows, SPAN):
        part = slice(start, start + SPAN)
        factor = dot32(tail[0, part, :], expand[...])
        weighted = (x_out[part, :].astype(jnp.float32) * factor).astype(jnp.bfloat16)
        gains.append(dot32(b_out[part, :], weighted, ((0,), (0,))))
    first_state[0] = gains[0]
    last_state[0, :STATE] = (gains[0] * pass_last[0] + gains[1]).astype(jnp.bfloat16)
    rest = jnp.broadcast_to(through[0], (HALO, WIDE))
    row = lax.broadcasted_iota(jnp.int32, (HALO, WIDE), 0)
    extra = jnp.zeros((HALO, WIDE), jnp.float32)
    for place in range(3):
        part = rest.astype(jnp.bfloat16).astype(jnp.float32)
        extra = jnp.where(row == place, part, extra)
        rest = rest - part
    last_state[0, STATE:] = extra.astype(jnp.bfloat16)


def mix_kernel(x_ref, b_ref, c_ref, decay_col, decay_row, step_row, seg_col, seg_row, out, scores):
    rows = x_ref.shape[0]
    lanes = lax.broadcasted_iota(jnp.int32, (SPAN, LANES), 1)
    for start in range(0, rows, SPAN):
        part = slice(start, start + SPAN)
        at_row = lax.broadcasted_iota(jnp.int32, (SPAN, SPAN), 0)
        at_col = lax.broadcasted_iota(jnp.int32, (SPAN, SPAN), 1)
        allowed = (seg_col[part, :] == seg_row[:, part]) & (at_row >= at_col)
        products = dot32(c_ref[part, :], b_ref[part, :], ((1,), (1,)))
        scores[...] = jnp.where(allowed, products, 0.0)
        for pair in range(PER_GROUP // 2):
            cols = slice(pair * LANES, (pair + 1) * LANES)
            values = x_ref[part, cols]
            halves = []
            for head in (2 * pair, 2 * pair + 1):
                spread = decay_col[0, part, head : head + 1] - decay_row[0, head : head + 1, part]
                mixing = (
                    scores[...] * jnp.exp(jnp.minimum(spread, 0.0)) * step_row[0, head : head + 1, part]
                ).astype(jnp.bfloat16)
                halves.append(dot32(mixing, values))
            out[part, cols] = jnp.where(lanes < HEAD_DIM, halves[0], halves[1])


def norm_kernel(inside, x_ref, c_ref, upper, lower, factor, expand, skip, gain, out, mixed):
    power = jnp.zeros((out.shape[0], 1), jnp.float32)
    for group in range(GROUPS):
        cols = slice(group * WIDE, (group + 1) * WIDE)
        c_mat = c_ref[:, group * STATE : (group + 1) * STATE]
        readout = dot32(c_mat, upper[0, group]) + dot32(c_mat, lower[0, group])
        total = inside[:, cols] + readout * dot32(factor[group], expand[...])
        total = total + x_ref[:, cols].astype(jnp.float32) * skip[:, cols]
        mixed[:, cols] = total
        power = power + jnp.sum(total * total, axis=1, keepdims=True)
    scale = lax.rsqrt(power / INNER + 1e-05)
    for group in range(GROUPS):
        cols = slice(group * WIDE, (group + 1) * WIDE)
        out[:, cols] = (mixed[:, cols] * scale * gain[:, cols]).astype(jnp.bfloat16)


def by_group(values):
    return values.reshape(values.shape[0], GROUPS, PER_GROUP).transpose(1, 0, 2)


def split_pair(values):
    grouped = by_group(values)
    upper = grouped.astype(jnp.bfloat16)
    lower = (grouped - upper.astype(jnp.float32)).astype(jnp.bfloat16)
    return jnp.concatenate([upper, lower], axis=2)


def along_lanes(values):
    return jnp.repeat(values, HEAD_DIM, axis=-1).reshape(values.shape[:-1] + (GROUPS, 1, WIDE))


def per_device(
    stream_tokens,
    xbc_weight,
    step_weight,
    conv_weight,
    conv_bias,
    step_bias,
    decay_rate,
    skip_gain,
    norm_gain,
    segment_ids,
    page_target,
):
    req_count = lax.axis_size("req")
    seq_count = lax.axis_size("seq")
    tok_rows = stream_tokens.shape[0]
    page_rows = tok_rows // req_count
    blocks = tok_rows // SPAN
    targets = page_target[0]
    spots = jnp.arange(req_count, dtype=jnp.int32)
    page_order = jnp.sum(jnp.where(targets[None, :] == spots[:, None], spots[None, :], 0), axis=1)
    params = pltpu.CompilerParams(vmem_limit_bytes=VMEM_LIMIT)

    pages = stream_tokens.reshape(req_count, page_rows, stream_tokens.shape[1])
    outgoing = jnp.take(pages, page_order, axis=0, mode="clip")
    tokens = lax.all_to_all(outgoing, "req", split_axis=0, concat_axis=0, tiled=True)
    tokens = tokens.reshape(tok_rows, stream_tokens.shape[1])
    prev_tokens = shifted(tokens[tok_rows - HALO :], "seq", 1)
    all_rows = jnp.concatenate([prev_tokens, tokens], axis=0)
    depth = xbc_weight.shape[0] // 2
    core = lax.rem(lax.axis_index("req"), 2)
    swap = [(i, i ^ 1) for i in range(req_count)]
    mine = lax.dynamic_slice_in_dim(xbc_weight, core * depth, depth, axis=0)
    given = lax.dynamic_slice_in_dim(xbc_weight, (1 - core) * depth, depth, axis=0)
    taken = lax.ppermute(given, "req", swap)
    chip_half = jnp.concatenate(
        [jnp.where(core == 0, mine, taken), jnp.where(core == 0, taken, mine)], axis=1
    )
    device_count = seq_count * req_count
    same_core = [list(range(first, device_count, 2)) for first in range(2)]
    near_half = lax.all_gather(
        chip_half, ("seq", "req"), axis=1, tiled=True, axis_index_groups=same_core
    )
    far_half = lax.ppermute(near_half, "req", swap)
    near_rows = lax.dynamic_slice_in_dim(all_rows, core * depth, depth, axis=1)
    far_rows = lax.dynamic_slice_in_dim(all_rows, (1 - core) * depth, depth, axis=1)
    raw_near = jnp.dot(near_rows, near_half, preferred_element_type=jnp.float32)
    raw_far = jnp.dot(far_rows, far_half, preferred_element_type=jnp.float32)
    raw_all = (raw_near + raw_far).astype(jnp.bfloat16)
    step_raw = jnp.dot(tokens, step_weight, preferred_element_type=jnp.float32).astype(jnp.bfloat16)

    seq_at = lax.axis_index("seq")
    full_ids = segment_ids[0]
    padded_ids = jnp.concatenate([jnp.full((KCONV - 1,), -1, jnp.int32), full_ids])
    labels = lax.dynamic_slice_in_dim(padded_ids, seq_at * tok_rows, tok_rows + KCONV - 1)
    seg_rows = labels[KCONV - 1 :]
    match = jnp.stack([labels[tap : tap + tok_rows] == seg_rows for tap in range(KCONV - 1)])
    match = jnp.broadcast_to(match.astype(jnp.float32)[:, :, None], (KCONV - 1, tok_rows, LANES))
    ends = seg_rows.reshape(blocks, SPAN)[:, SPAN - 1]
    before = jnp.concatenate([labels[KCONV - 2 : KCONV - 1], ends[:-1]])

    step_size = jax.nn.softplus(step_raw.astype(jnp.float32) + step_bias[None, :])
    log_decay = jnp.cumsum(
        (-step_size * decay_rate[None, :]).reshape(blocks, SPAN, HEADS), axis=1
    )
    last_decay = log_decay[:, SPAN - 1]
    seg_blocks = seg_rows.reshape(blocks, SPAN)
    keep = (seg_blocks == before[:, None])[:, :, None]
    factor = split_pair(jnp.where(keep, jnp.exp(log_decay), 0.0).reshape(tok_rows, HEADS))
    in_tail = (seg_blocks == ends[:, None])[:, :, None]
    tail = jnp.where(in_tail, jnp.exp(last_decay[:, None] - log_decay), 0.0).reshape(tok_rows, HEADS)
    tail = split_pair(tail * step_size)
    passing = jnp.where((ends == before)[:, None], jnp.exp(last_decay), 0.0)
    through = along_lanes(passing[0] * passing[1])
    passing = along_lanes(passing)
    flat_decay = log_decay.reshape(tok_rows, HEADS)
    decay_col = by_group(flat_decay)
    decay_row = flat_decay.T.reshape(GROUPS, PER_GROUP, tok_rows)
    step_row = step_size.T.reshape(GROUPS, PER_GROUP, tok_rows)
    owner = jnp.arange(WIDE) // HEAD_DIM
    expand = (owner[None, :] == (jnp.arange(2 * PER_GROUP) % PER_GROUP)[:, None]).astype(
        jnp.bfloat16
    )

    bias_row = conv_bias[None, :]
    at_b = INNER // STATE
    at_c = at_b + GROUPS
    raw_len = tok_rows + HALO

    def columns(height, width, at):
        return pl.BlockSpec((height, width), lambda group: (0, at + group))

    def of_group(*shape):
        return pl.BlockSpec((1,) + shape, lambda group: (group, 0, 0))

    def whole(*shape):
        return pl.BlockSpec(shape, lambda step: (0,) * len(shape))

    x_all, b_all, c_all, first_state, last_state = pl.pallas_call(
        conv_kernel,
        grid=(GROUPS,),
        in_specs=[
            columns(raw_len, WIDE, 0),
            columns(raw_len, STATE, at_b),
            columns(raw_len, STATE, at_c),
            columns(KCONV, WIDE, 0),
            columns(KCONV, STATE, at_b),
            columns(KCONV, STATE, at_c),
            columns(1, WIDE, 0),
            columns(1, STATE, at_b),
            columns(1, STATE, at_c),
            whole(KCONV - 1, tok_rows, LANES),
            of_group(tok_rows, 2 * PER_GROUP),
            of_group(1, WIDE),
            of_group(1, WIDE),
            whole(2 * PER_GROUP, WIDE),
        ],
        out_specs=[
            columns(tok_rows, WIDE, 0),
            columns(tok_rows, STATE, 0),
            columns(tok_rows, STATE, 0),
            of_group(STATE, WIDE),
            of_group(STATE + HALO, WIDE),
        ],
        out_shape=[
            jax.ShapeDtypeStruct((tok_rows, INNER), jnp.bfloat16),
            jax.ShapeDtypeStruct((tok_rows, GROUPS * STATE), jnp.bfloat16),
            jax.ShapeDtypeStruct((tok_rows, GROUPS * STATE), jnp.bfloat16),
            jax.ShapeDtypeStruct((GROUPS, STATE, WIDE), jnp.float32),
            jax.ShapeDtypeStruct((GROUPS, STATE + HALO, WIDE), jnp.bfloat16),
        ],
        scratch_shapes=[pltpu.VMEM((raw_len, WIDE), jnp.float32)],
        compiler_params=params,
        cost_estimate=pl.CostEstimate(
            flops=2 * tok_rows * INNER * STATE, bytes_accessed=14 << 20, transcendentals=tok_rows * XBC
        ),
    )(
        raw_all, raw_all, raw_all, conv_weight, conv_weight, conv_weight,
        bias_row, bias_row, bias_row, match, tail, passing[1], through, expand,
    )
    all_states = lax.all_gather(last_state, "seq")

    inside = pl.pallas_call(
        mix_kernel,
        grid=(GROUPS,),
        in_specs=[
            columns(tok_rows, WIDE, 0),
            columns(tok_rows, STATE, 0),
            columns(tok_rows, STATE, 0),
            of_group(tok_rows, PER_GROUP),
            of_group(PER_GROUP, tok_rows),
            of_group(PER_GROUP, tok_rows),
            whole(tok_rows, 1),
            whole(1, tok_rows),
        ],
        out_specs=columns(tok_rows, WIDE, 0),
        out_shape=jax.ShapeDtypeStruct((tok_rows, INNER), jnp.float32),
        scratch_shapes=[pltpu.VMEM((SPAN, SPAN), jnp.float32)],
        compiler_params=params,
        cost_estimate=pl.CostEstimate(
            flops=16 * tok_rows * SPAN * INNER,
            bytes_accessed=14 << 20,
            transcendentals=tok_rows * SPAN * HEADS,
        ),
    )(x_all, b_all, c_all, decay_col, decay_row, step_row, seg_rows[:, None], seg_rows[None, :])

    all_through = jnp.sum(all_states[:, :, STATE : STATE + 3].astype(jnp.float32), axis=2, keepdims=True)
    running = jnp.ones((GROUPS, 1, WIDE), jnp.float32)
    incoming = jnp.zeros((GROUPS, STATE, WIDE), jnp.float32)
    for turn in range(seq_count - 2, -1, -1):
        share = jnp.where(turn < seq_at, running, 0.0)
        incoming = incoming + share * all_states[turn, :, :STATE].astype(jnp.float32)
        running = jnp.where(turn < seq_at, running * all_through[turn], running)
    states = jnp.stack([incoming, passing[0] * incoming + first_state])
    upper = states.astype(jnp.bfloat16)
    lower = (states - upper.astype(jnp.float32)).astype(jnp.bfloat16)

    tile = SPAN // 2
    per_block = SPAN // tile
    normed = pl.pallas_call(
        norm_kernel,
        grid=(tok_rows // tile,),
        in_specs=[
            pl.BlockSpec((tile, INNER), lambda step: (step, 0)),
            pl.BlockSpec((tile, INNER), lambda step: (step, 0)),
            pl.BlockSpec((tile, GROUPS * STATE), lambda step: (step, 0)),
            pl.BlockSpec((1, GROUPS, STATE, WIDE), lambda step: (step // per_block, 0, 0, 0)),
            pl.BlockSpec((1, GROUPS, STATE, WIDE), lambda step: (step // per_block, 0, 0, 0)),
            pl.BlockSpec((GROUPS, tile, 2 * PER_GROUP), lambda step: (0, step, 0)),
            whole(2 * PER_GROUP, WIDE),
            whole(1, INNER),
            whole(1, INNER),
        ],
        out_specs=pl.BlockSpec((tile, INNER), lambda step: (step, 0)),
        out_shape=jax.ShapeDtypeStruct((tok_rows, INNER), jnp.bfloat16),
        scratch_shapes=[pltpu.VMEM((tile, INNER), jnp.float32)],
        compiler_params=params,
        cost_estimate=pl.CostEstimate(
            flops=4 * tok_rows * INNER * STATE, bytes_accessed=22 << 20, transcendentals=tok_rows
        ),
    )(
        inside, x_all, c_all, upper, lower, factor, expand,
        jnp.repeat(skip_gain, HEAD_DIM)[None, :], norm_gain[None, :],
    )
    returned = lax.all_to_all(
        normed.reshape(req_count, page_rows, INNER), "req", split_axis=0, concat_axis=0, tiled=True
    )
    return jnp.take(returned, targets, axis=0, mode="clip").reshape(tok_rows, INNER)


def solution(mesh):
    in_specs = (
        P(("seq", "req"), None),
        P(None, ("seq", "req")),
        P(),
        P(),
        P(),
        P(),
        P(),
        P(),
        P(),
        P("req", None),
        P(("seq", "req"), None),
    )
    out_specs = P(("seq", "req"), None)
    return jax.shard_map(
        per_device, mesh=mesh, in_specs=in_specs, out_specs=out_specs, check_vma=False
    )
```

```python
from functools import partial

import jax
import jax.numpy as jnp
from jax import lax
from jax.experimental import pallas as pl
from jax.experimental.pallas import tpu as pltpu
from jax.sharding import PartitionSpec as P

HEADS = 64
HEAD_DIM = 64
GROUPS = 4
STATE = 128
KCONV = 4
SPAN = 256
INNER = 4096
XBC = 5120


def shifted(shard, axis, by):
    peers = lax.axis_size(axis)
    pairs = [(i, i + by) for i in range(peers) if 0 <= i + by < peers]
    return lax.ppermute(shard, axis, pairs)


HALO = 16
PER_GROUP = HEADS // GROUPS
WIDE = PER_GROUP * HEAD_DIM
LANES = 128
VMEM_LIMIT = 40 * 1024 * 1024


def dot32(left, right, contract=((1,), (0,))):
    return lax.dot_general(left, right, (contract, ((), ())), preferred_element_type=jnp.float32)


def conv_kernel(
    raw_x, raw_b, raw_c, w_x, w_b, w_c, bias_x, bias_b, bias_c, match, tail, pass_last, through, expand,
    x_out, b_out, c_out, first_state, last_state, wide,
):
    rows = x_out.shape[0]
    piece = 64

    def conv(raw, weight, bias, out):
        wide[:, : raw.shape[1]] = raw[...].astype(jnp.float32)

        @pl.loop(0, raw.shape[1] // LANES)
        def _(chunk):
            cols = pl.ds(pl.multiple_of(chunk * LANES, LANES), LANES)
            taps = weight[:, cols]
            shift = bias[:, cols]
            for start in range(0, rows, piece):
                base = HALO + start
                total = shift + taps[KCONV - 1 : KCONV] * wide[base : base + piece, cols]
                for tap in range(KCONV - 1):
                    low = base - (KCONV - 1) + tap
                    total = total + (
                        taps[tap : tap + 1]
                        * wide[low : low + piece, cols]
                        * match[tap, start : start + piece, :]
                    )
                out[start : start + piece, cols] = (total / (1.0 + jnp.exp(-total))).astype(
                    jnp.bfloat16
                )

    conv(raw_x, w_x, bias_x, x_out)
    conv(raw_b, w_b, bias_b, b_out)
    conv(raw_c, w_c, bias_c, c_out)
    gains = []
    for start in range(0, rows, SPAN):
        part = slice(start, start + SPAN)
        factor = dot32(tail[0, part, :], expand[...])
        weighted = (x_out[part, :].astype(jnp.float32) * factor).astype(jnp.bfloat16)
        gains.append(dot32(b_out[part, :], weighted, ((0,), (0,))))
    first_state[0] = gains[0]
    last_state[0, :STATE] = (gains[0] * pass_last[0] + gains[1]).astype(jnp.bfloat16)
    rest = jnp.broadcast_to(through[0], (HALO, WIDE))
    row = lax.broadcasted_iota(jnp.int32, (HALO, WIDE), 0)
    extra = jnp.zeros((HALO, WIDE), jnp.float32)
    for place in range(3):
        part = rest.astype(jnp.bfloat16).astype(jnp.float32)
        extra = jnp.where(row == place, part, extra)
        rest = rest - part
    last_state[0, STATE:] = extra.astype(jnp.bfloat16)


def mix_kernel(x_ref, b_ref, c_ref, decay_col, decay_row, step_row, seg_col, seg_row, out, scores):
    rows = x_ref.shape[0]
    lanes = lax.broadcasted_iota(jnp.int32, (SPAN, LANES), 1)
    for start in range(0, rows, SPAN):
        part = slice(start, start + SPAN)
        at_row = lax.broadcasted_iota(jnp.int32, (SPAN, SPAN), 0)
        at_col = lax.broadcasted_iota(jnp.int32, (SPAN, SPAN), 1)
        allowed = (seg_col[part, :] == seg_row[:, part]) & (at_row >= at_col)
        products = dot32(c_ref[part, :], b_ref[part, :], ((1,), (1,)))
        scores[...] = jnp.where(allowed, products, 0.0)
        for pair in range(PER_GROUP // 2):
            cols = slice(pair * LANES, (pair + 1) * LANES)
            values = x_ref[part, cols]
            halves = []
            for head in (2 * pair, 2 * pair + 1):
                spread = decay_col[0, part, head : head + 1] - decay_row[0, head : head + 1, part]
                mixing = (
                    scores[...] * jnp.exp(jnp.minimum(spread, 0.0)) * step_row[0, head : head + 1, part]
                ).astype(jnp.bfloat16)
                halves.append(dot32(mixing, values))
            out[part, cols] = jnp.where(lanes < HEAD_DIM, halves[0], halves[1])


def norm_kernel(inside, x_ref, c_ref, upper, lower, factor, expand, skip, gain, out, mixed):
    power = jnp.zeros((out.shape[0], 1), jnp.float32)
    for group in range(GROUPS):
        cols = slice(group * WIDE, (group + 1) * WIDE)
        c_mat = c_ref[:, group * STATE : (group + 1) * STATE]
        readout = dot32(c_mat, upper[0, group]) + dot32(c_mat, lower[0, group])
        total = inside[:, cols] + readout * dot32(factor[group], expand[...])
        total = total + x_ref[:, cols].astype(jnp.float32) * skip[:, cols]
        mixed[:, cols] = total
        power = power + jnp.sum(total * total, axis=1, keepdims=True)
    scale = lax.rsqrt(power / INNER + 1e-05)
    for group in range(GROUPS):
        cols = slice(group * WIDE, (group + 1) * WIDE)
        out[:, cols] = (mixed[:, cols] * scale * gain[:, cols]).astype(jnp.bfloat16)


def by_group(values):
    return values.reshape(values.shape[0], GROUPS, PER_GROUP).transpose(1, 0, 2)


def split_pair(values):
    grouped = by_group(values)
    upper = grouped.astype(jnp.bfloat16)
    lower = (grouped - upper.astype(jnp.float32)).astype(jnp.bfloat16)
    return jnp.concatenate([upper, lower], axis=2)


def along_lanes(values):
    return jnp.repeat(values, HEAD_DIM, axis=-1).reshape(values.shape[:-1] + (GROUPS, 1, WIDE))


def per_device(
    stream_tokens,
    xbc_weight,
    step_weight,
    conv_weight,
    conv_bias,
    step_bias,
    decay_rate,
    skip_gain,
    norm_gain,
    segment_ids,
    page_target,
):
    req_count = lax.axis_size("req")
    seq_count = lax.axis_size("seq")
    tok_rows = stream_tokens.shape[0]
    page_rows = tok_rows // req_count
    blocks = tok_rows // SPAN
    targets = page_target[0]
    spots = jnp.arange(req_count, dtype=jnp.int32)
    page_order = jnp.sum(jnp.where(targets[None, :] == spots[:, None], spots[None, :], 0), axis=1)
    params = pltpu.CompilerParams(vmem_limit_bytes=VMEM_LIMIT)

    pages = stream_tokens.reshape(req_count, page_rows, stream_tokens.shape[1])
    outgoing = jnp.take(pages, page_order, axis=0, mode="clip")
    tokens = lax.all_to_all(outgoing, "req", split_axis=0, concat_axis=0, tiled=True)
    tokens = tokens.reshape(tok_rows, stream_tokens.shape[1])
    prev_tokens = shifted(tokens[tok_rows - HALO :], "seq", 1)
    all_rows = jnp.concatenate([prev_tokens, tokens], axis=0)
    full_weight = lax.all_gather(xbc_weight, ("seq", "req"), axis=1, tiled=True)
    raw_all = jnp.dot(all_rows, full_weight, preferred_element_type=jnp.float32).astype(
        jnp.bfloat16
    )
    step_raw = jnp.dot(tokens, step_weight, preferred_element_type=jnp.float32).astype(jnp.bfloat16)

    seq_at = lax.axis_index("seq")
    full_ids = segment_ids[0]
    padded_ids = jnp.concatenate([jnp.full((KCONV - 1,), -1, jnp.int32), full_ids])
    labels = lax.dynamic_slice_in_dim(padded_ids, seq_at * tok_rows, tok_rows + KCONV - 1)
    seg_rows = labels[KCONV - 1 :]
    match = jnp.stack([labels[tap : tap + tok_rows] == seg_rows for tap in range(KCONV - 1)])
    match = jnp.broadcast_to(match.astype(jnp.float32)[:, :, None], (KCONV - 1, tok_rows, LANES))
    ends = seg_rows.reshape(blocks, SPAN)[:, SPAN - 1]
    before = jnp.concatenate([labels[KCONV - 2 : KCONV - 1], ends[:-1]])

    step_size = jax.nn.softplus(step_raw.astype(jnp.float32) + step_bias[None, :])
    log_decay = jnp.cumsum(
        (-step_size * decay_rate[None, :]).reshape(blocks, SPAN, HEADS), axis=1
    )
    last_decay = log_decay[:, SPAN - 1]
    seg_blocks = seg_rows.reshape(blocks, SPAN)
    keep = (seg_blocks == before[:, None])[:, :, None]
    factor = split_pair(jnp.where(keep, jnp.exp(log_decay), 0.0).reshape(tok_rows, HEADS))
    in_tail = (seg_blocks == ends[:, None])[:, :, None]
    tail = jnp.where(in_tail, jnp.exp(last_decay[:, None] - log_decay), 0.0).reshape(tok_rows, HEADS)
    tail = split_pair(tail * step_size)
    passing = jnp.where((ends == before)[:, None], jnp.exp(last_decay), 0.0)
    through = along_lanes(passing[0] * passing[1])
    passing = along_lanes(passing)
    flat_decay = log_decay.reshape(tok_rows, HEADS)
    decay_col = by_group(flat_decay)
    decay_row = flat_decay.T.reshape(GROUPS, PER_GROUP, tok_rows)
    step_row = step_size.T.reshape(GROUPS, PER_GROUP, tok_rows)
    owner = jnp.arange(WIDE) // HEAD_DIM
    expand = (owner[None, :] == (jnp.arange(2 * PER_GROUP) % PER_GROUP)[:, None]).astype(
        jnp.bfloat16
    )

    bias_row = conv_bias[None, :]
    at_b = INNER // STATE
    at_c = at_b + GROUPS
    raw_len = tok_rows + HALO

    def columns(height, width, at):
        return pl.BlockSpec((height, width), lambda group: (0, at + group))

    def of_group(*shape):
        return pl.BlockSpec((1,) + shape, lambda group: (group, 0, 0))

    def whole(*shape):
        return pl.BlockSpec(shape, lambda step: (0,) * len(shape))

    x_all, b_all, c_all, first_state, last_state = pl.pallas_call(
        conv_kernel,
        grid=(GROUPS,),
        in_specs=[
            columns(raw_len, WIDE, 0),
            columns(raw_len, STATE, at_b),
            columns(raw_len, STATE, at_c),
            columns(KCONV, WIDE, 0),
            columns(KCONV, STATE, at_b),
            columns(KCONV, STATE, at_c),
            columns(1, WIDE, 0),
            columns(1, STATE, at_b),
            columns(1, STATE, at_c),
            whole(KCONV - 1, tok_rows, LANES),
            of_group(tok_rows, 2 * PER_GROUP),
            of_group(1, WIDE),
            of_group(1, WIDE),
            whole(2 * PER_GROUP, WIDE),
        ],
        out_specs=[
            columns(tok_rows, WIDE, 0),
            columns(tok_rows, STATE, 0),
            columns(tok_rows, STATE, 0),
            of_group(STATE, WIDE),
            of_group(STATE + HALO, WIDE),
        ],
        out_shape=[
            jax.ShapeDtypeStruct((tok_rows, INNER), jnp.bfloat16),
            jax.ShapeDtypeStruct((tok_rows, GROUPS * STATE), jnp.bfloat16),
            jax.ShapeDtypeStruct((tok_rows, GROUPS * STATE), jnp.bfloat16),
            jax.ShapeDtypeStruct((GROUPS, STATE, WIDE), jnp.float32),
            jax.ShapeDtypeStruct((GROUPS, STATE + HALO, WIDE), jnp.bfloat16),
        ],
        scratch_shapes=[pltpu.VMEM((raw_len, WIDE), jnp.float32)],
        compiler_params=params,
        cost_estimate=pl.CostEstimate(
            flops=2 * tok_rows * INNER * STATE, bytes_accessed=14 << 20, transcendentals=tok_rows * XBC
        ),
    )(
        raw_all, raw_all, raw_all, conv_weight, conv_weight, conv_weight,
        bias_row, bias_row, bias_row, match, tail, passing[1], through, expand,
    )
    earlier = [shifted(last_state, "seq", by) for by in range(1, seq_count)]

    inside = pl.pallas_call(
        mix_kernel,
        grid=(GROUPS,),
        in_specs=[
            columns(tok_rows, WIDE, 0),
            columns(tok_rows, STATE, 0),
            columns(tok_rows, STATE, 0),
            of_group(tok_rows, PER_GROUP),
            of_group(PER_GROUP, tok_rows),
            of_group(PER_GROUP, tok_rows),
            whole(tok_rows, 1),
            whole(1, tok_rows),
        ],
        out_specs=columns(tok_rows, WIDE, 0),
        out_shape=jax.ShapeDtypeStruct((tok_rows, INNER), jnp.float32),
        scratch_shapes=[pltpu.VMEM((SPAN, SPAN), jnp.float32)],
        compiler_params=params,
        cost_estimate=pl.CostEstimate(
            flops=16 * tok_rows * SPAN * INNER,
            bytes_accessed=14 << 20,
            transcendentals=tok_rows * SPAN * HEADS,
        ),
    )(x_all, b_all, c_all, decay_col, decay_row, step_row, seg_rows[:, None], seg_rows[None, :])

    running = jnp.ones((GROUPS, 1, WIDE), jnp.float32)
    incoming = jnp.zeros((GROUPS, STATE, WIDE), jnp.float32)
    for arrived in earlier:
        incoming = incoming + running * arrived[:, :STATE].astype(jnp.float32)
        decays = arrived[:, STATE : STATE + 3].astype(jnp.float32)
        running = running * jnp.sum(decays, axis=1, keepdims=True)
    states = jnp.stack([incoming, passing[0] * incoming + first_state])
    upper = states.astype(jnp.bfloat16)
    lower = (states - upper.astype(jnp.float32)).astype(jnp.bfloat16)

    tile = SPAN // 2
    per_block = SPAN // tile
    normed = pl.pallas_call(
        norm_kernel,
        grid=(tok_rows // tile,),
        in_specs=[
            pl.BlockSpec((tile, INNER), lambda step: (step, 0)),
            pl.BlockSpec((tile, INNER), lambda step: (step, 0)),
            pl.BlockSpec((tile, GROUPS * STATE), lambda step: (step, 0)),
            pl.BlockSpec((1, GROUPS, STATE, WIDE), lambda step: (step // per_block, 0, 0, 0)),
            pl.BlockSpec((1, GROUPS, STATE, WIDE), lambda step: (step // per_block, 0, 0, 0)),
            pl.BlockSpec((GROUPS, tile, 2 * PER_GROUP), lambda step: (0, step, 0)),
            whole(2 * PER_GROUP, WIDE),
            whole(1, INNER),
            whole(1, INNER),
        ],
        out_specs=pl.BlockSpec((tile, INNER), lambda step: (step, 0)),
        out_shape=jax.ShapeDtypeStruct((tok_rows, INNER), jnp.bfloat16),
        scratch_shapes=[pltpu.VMEM((tile, INNER), jnp.float32)],
        compiler_params=params,
        cost_estimate=pl.CostEstimate(
            flops=4 * tok_rows * INNER * STATE, bytes_accessed=22 << 20, transcendentals=tok_rows
        ),
    )(
        inside, x_all, c_all, upper, lower, factor, expand,
        jnp.repeat(skip_gain, HEAD_DIM)[None, :], norm_gain[None, :],
    )
    returned = lax.all_to_all(
        normed.reshape(req_count, page_rows, INNER), "req", split_axis=0, concat_axis=0, tiled=True
    )
    return jnp.take(returned, targets, axis=0, mode="clip").reshape(tok_rows, INNER)


def solution(mesh):
    in_specs = (
        P(("seq", "req"), None),
        P(None, ("seq", "req")),
        P(),
        P(),
        P(),
        P(),
        P(),
        P(),
        P(),
        P("req", None),
        P(("seq", "req"), None),
    )
    out_specs = P(("seq", "req"), None)
    return jax.shard_map(
        per_device, mesh=mesh, in_specs=in_specs, out_specs=out_specs, check_vma=False
    )
```
